32 devices in a mesh: lon: 8 (over z, core), lat: 4 (over y, x).
Axes of the slice: x: 2, y: 2, z: 4, core: 2. Of those that a mesh axis runs over, the one named last changes fastest.
Arguments:
- latent: bfloat16 [96, 192, 512], P('lat', 'lon'), may hold values from -24 to 24
- ln1_gain: float32 [512], replicated, may hold values from 0.1 to 1.9
- qkv_weight: bfloat16 [512, 1536], replicated, may hold values from -0.25 to 0.25
- qkv_bias: float32 [1536], replicated, may hold values from -3 to 3
- bias_table: float32 [253, 8], replicated, may hold values from -4 to 242
- bias_index: int32 [72, 72], replicated, may hold values from 0 to 252
- proj_weight: bfloat16 [512, 512], replicated, may hold values from -0.25 to 0.25
- ln2_gain: float32 [512], replicated, may hold values from 0.1 to 1.9
- fc1_weight: bfloat16 [512, 2048], replicated, may hold values from -0.25 to 0.25
- fc1_bias: float32 [2048], replicated, may hold values from -3 to 3
- fc2_weight: bfloat16 [2048, 512], replicated, may hold values from -0.125 to 0.125
- merge_gain: float32 [2048], replicated, may hold values from 0.1 to 1.9
- reduce_weight: bfloat16 [2048, 1024], replicated, may hold values from -0.125 to 0.125
Outputs:
- coarse: bfloat16 [48, 96, 1024], P('lat', 'lon')
The draws below stay inside these ranges and needn't reach their ends.
All inputs are finite; a program needn't handle non-finite values.
Results may differ from the reference program's by a relative error of at most 0.017.
Values may be sent and summed in bfloat16 or wider, within the bound.
A program may use at most 64 MiB of HBM per device.

```python
import jax
import jax.numpy as jnp
from jax import lax

D = 512
HEADS = 8
FF = 2048
WH = 6
WW = 12
SH = 3
SW = 6
WT = 72
NB = 253
H = 96
W = 192


def draw_latent(key, part):
    keys = jax.random.split(jax.random.fold_in(key, 11), 1)
    base = jnp.clip(jax.random.normal(keys[0], (H, W, D), jnp.float32), -6.0, 6.0)
    values = base
    return values.astype(jnp.bfloat16)


def draw_bias_table(key, part):
    keys = jax.random.split(jax.random.fold_in(key, 23), 1)
    values = jnp.clip(jax.random.normal(keys[0], (NB, HEADS), jnp.float32), -4.0, 4.0)
    return values.astype(jnp.float32)


def plant(values, stream_key, low, high):
    shape = values.shape
    index_at = [jax.random.randint(jax.random.fold_in(stream_key, axis), (), 0, shape[axis]) for axis in range(len(shape))]
    values = values.at[tuple(index_at)].set(low)
    longest = shape.index(max(shape))
    index_at[longest] = (index_at[longest] + 1) % shape[longest]
    return values.at[tuple(index_at)].set(high)


def noise(stream_key, shape, scale, limit, held_as=jnp.bfloat16):
    return jnp.clip(scale * jax.random.normal(stream_key, shape, jnp.float32), -limit, limit).astype(held_as)


def setup_inputs(seed: int = 0) -> dict:
    key_list = jax.random.split(jax.random.key(seed), 14)
    return {
        "latent": draw_latent(jax.random.fold_in(key_list[13], 71), 0),
        "ln1_gain": jnp.clip(1.0 + 0.18 * jax.random.normal(key_list[1], (D,), jnp.float32), 0.1, 1.9),
        "qkv_weight": noise(key_list[2], (D, 3 * D), D ** -0.5, 0.25),
        "qkv_bias": noise(key_list[3], (3 * D,), 0.5, 3.0, jnp.float32),
        "bias_table": draw_bias_table(jax.random.fold_in(key_list[13], 71), 0),
        "bias_index": plant(jax.random.randint(key_list[5], (WT, WT), 0, NB), jax.random.fold_in(key_list[5], 1), 0, NB - 1).astype(jnp.int32),
        "proj_weight": noise(key_list[6], (D, D), D ** -0.5, 0.25),
        "ln2_gain": jnp.clip(1.0 + 0.18 * jax.random.normal(key_list[7], (D,), jnp.float32), 0.1, 1.9),
        "fc1_weight": noise(key_list[8], (D, FF), D ** -0.5, 0.25),
        "fc1_bias": noise(key_list[9], (FF,), 0.5, 3.0, jnp.float32),
        "fc2_weight": noise(key_list[10], (FF, D), FF ** -0.5, 0.125),
        "merge_gain": jnp.clip(1.0 + 0.18 * jax.random.normal(key_list[11], (4 * D,), jnp.float32), 0.1, 1.9),
        "reduce_weight": noise(key_list[12], (4 * D, 2 * D), (4 * D) ** -0.5, 0.125),
    }


EPSILON = 1e-05
MASKED = -1e+30

def layer_norm(values, gain):
    values = values.astype(jnp.float32)
    center = values - lax.optimization_barrier(jnp.mean(values, axis=-1, keepdims=True))
    spread = lax.optimization_barrier(jnp.mean(center * center, axis=-1, keepdims=True))
    return center * lax.rsqrt(spread + EPSILON) * gain

def window_attention(qkv_windows, bias, allowed, head_count):
    window_count, window_tokens, triple = qkv_windows.shape
    model_dim = triple // 3
    head_size = model_dim // head_count
    pieces = qkv_windows.astype(jnp.float32).reshape(window_count, window_tokens, 3, head_count, head_size)
    scores = jnp.einsum('wqhc,wkhc->whqk', pieces[:, :, 0], pieces[:, :, 1])
    scores = scores * head_size ** (-0.5) + bias
    scores = jnp.where(allowed, scores, MASKED)
    weights = jax.nn.softmax(scores, axis=-1).astype(jnp.bfloat16)
    mixed = jnp.einsum('whqk,wkhc->wqhc', weights.astype(jnp.float32), pieces[:, :, 2])
    return mixed.reshape(window_count, window_tokens, model_dim).astype(jnp.bfloat16)

def reference(latent, ln1_gain, qkv_weight, qkv_bias, bias_table, bias_index, proj_weight, ln2_gain, fc1_weight, fc1_bias, fc2_weight, merge_gain, reduce_weight):
    grid_rows, grid_cols, model_dim = latent.shape
    head_count = bias_table.shape[1]
    window_tokens = WH * WW
    strips = grid_cols // WW
    table = jnp.transpose(bias_table[bias_index], (2, 0, 1))
    normed = layer_norm(latent, ln1_gain).astype(jnp.bfloat16)
    shifted = jnp.roll(normed, (-SH, -SW), axis=(0, 1))
    bands = shifted.reshape(grid_rows // WH, WH, grid_cols, model_dim)
    offsets = (jnp.arange(window_tokens, dtype=jnp.int32) // WW).astype(jnp.int32)

    def attend(operands):
        band, start = operands
        region = start + offsets >= grid_rows - SH
        allowed = (region[:, None] == region[None, :])[None, None]
        windows = band.reshape(WH, strips, WW, model_dim).transpose(1, 0, 2, 3).reshape(-1, model_dim)
        qkv = jnp.dot(windows, qkv_weight, preferred_element_type=jnp.float32) + qkv_bias
        qkv = qkv.astype(jnp.bfloat16).reshape(strips, window_tokens, 3 * model_dim)
        mixed = window_attention(qkv, table, allowed, head_count)
        result = jnp.dot(mixed.reshape(-1, model_dim), proj_weight, preferred_element_type=jnp.float32).astype(jnp.bfloat16)
        return result.reshape(strips, WH, WW, model_dim).transpose(1, 0, 2, 3).reshape(WH, grid_cols, model_dim)
    starts = (jnp.arange(grid_rows // WH, dtype=jnp.int32) * WH).astype(jnp.int32)
    attended = lax.map(attend, (bands, starts)).reshape(grid_rows, grid_cols, model_dim)
    attention_out = jnp.roll(attended, (SH, SW), axis=(0, 1))

    def finish(operands):
        latent_band, attn_band = operands
        hidden = latent_band.astype(jnp.float32) + attn_band.astype(jnp.float32)
        normed_two = layer_norm(hidden, ln2_gain).astype(jnp.bfloat16).reshape(-1, model_dim)
        inner = jax.nn.gelu(jnp.dot(normed_two, fc1_weight, preferred_element_type=jnp.float32) + fc1_bias, approximate=False).astype(jnp.bfloat16)
        block = (hidden.reshape(-1, model_dim) + jnp.dot(inner, fc2_weight, preferred_element_type=jnp.float32)).astype(jnp.bfloat16)
        quads = block.reshape(WH // 2, 2, grid_cols // 2, 2, model_dim).transpose(0, 2, 3, 1, 4).reshape(WH // 2, grid_cols // 2, 4 * model_dim)
        merged = layer_norm(quads, merge_gain).astype(jnp.bfloat16)
        result = jnp.dot(merged.reshape(-1, 4 * model_dim), reduce_weight, preferred_element_type=jnp.float32)
        return result.astype(jnp.bfloat16).reshape(WH // 2, grid_cols // 2, 2 * model_dim)
    coarse = lax.map(finish, (latent.reshape(grid_rows // WH, WH, grid_cols, model_dim), attention_out.reshape(grid_rows // WH, WH, grid_cols, model_dim)))
    return coarse.reshape(grid_rows // 2, grid_cols // 2, 2 * model_dim)
```

```python
import functools

import jax
import jax.numpy as jnp
import numpy as np
from jax import lax
from jax.experimental import pallas as pl
from jax.experimental.pallas import tpu as pltpu
from jax.sharding import PartitionSpec as P

WH = 6
WW = 12
SH = 3
SW = 6
WT = WH * WW
WP = 80

EPSILON = 1e-05
MASKED = -1e30
MESH = pl.DeviceIdType.MESH


def up16(n):
    return (n + 15) // 16 * 16


def one_hot(rows, cols, pairs):
    out = np.zeros((rows, cols), np.float32)
    for r, c in pairs:
        out[r, c] = 1.0
    return out.astype(jnp.bfloat16)


@functools.lru_cache(None)
def plan(tr, tc):
    nb, nc = tr // WH, tc // WW
    windows = [(b, c) for b in range(nb - 1) for c in range(nc - 1)]
    inner = len(windows)
    windows += [(b, nc - 1) for b in range(nb - 1)]
    windows += [(nb - 1, c) for c in range(nc)]
    slot = {}
    for w, (b, c) in enumerate(windows):
        for r in range(WH):
            for k in range(WW):
                slot[b * WH + r, c * WW + k] = w * WP + r * WW + k
    east = [(i, j) for i in range(SH, tr) for j in range(SW)]
    south = [(i, j) for i in range(SH) for j in range(SW, tc)]
    corner = [(i, j) for i in range(SH) for j in range(SW)]
    sizes = [up16(len(x)) for x in (east, south, corner)]
    starts = [0, sizes[0], sizes[0] + sizes[1]]
    halo = sum(sizes)
    packed = {}
    for s, x in zip(starts, (east, south, corner)):
        for n, cell in enumerate(x):
            packed[cell] = s + n
    own = tr * tc
    pack = one_hot(halo, own, [(v, i * tc + j) for (i, j), v in packed.items()])
    rows = len(windows) * WP
    p_lat, p_halo, back = [], [], []
    for (i, j), s in slot.items():
        gi, gj = i + SH, j + SW
        wi, wj = gi % tr, gj % tc
        if gi < tr and gj < tc:
            p_lat.append((s, gi * tc + gj))
        else:
            p_halo.append((s, packed[wi, wj]))
            back.append((packed[wi, wj], s - inner * WP))
    p_lat = one_hot(rows, own, p_lat)
    p_halo = one_hot(rows, halo, p_halo)[inner * WP:]
    back = one_hot(halo, rows - inner * WP, back)
    first_r, first_c = -(-SH // 2), -(-SW // 2)
    cells = [(a, b) for a in range(tr // 2) for b in range(tc // 2)]
    free = [x for x in cells if x[0] >= first_r and x[1] >= first_c]
    n1 = len(free) // 16 * 16
    order = free + [x for x in cells if x not in set(free)]
    n2 = len(order) - n1
    f_lat, f_att, f_ret = [], [], []
    for n, (a, b) in enumerate(order):
        for q in range(4):
            i, j = 2 * a + q % 2, 2 * b + q // 2
            t = q * n1 + n if n < n1 else 4 * n1 + q * n2 + n - n1
            f_lat.append((t, i * tc + j))
            if i >= SH and j >= SW:
                f_att.append((t, slot[i - SH, j - SW]))
            else:
                f_ret.append((t - 4 * n1, packed[i, j]))
    f_lat = one_hot(own, own, f_lat)
    f_att = one_hot(own, rows, f_att)
    f_ret = one_hot(4 * n2, halo, f_ret)
    wide = up16(tc // 2)
    out = one_hot(tr // 2 * wide, len(order), [(a * wide + b, n) for n, (a, b) in enumerate(order)])
    mats = dict(pack=pack, p_lat=p_lat, p_halo=p_halo, back=back, f_lat=f_lat, f_att=f_att, f_ret=f_ret, out=out)
    return mats, len(windows), inner, nc, sizes, starts, n1, n2, wide


def norm(values, gain):
    center = values - jnp.mean(values, axis=-1, keepdims=True)
    spread = jnp.mean(center * center, axis=-1, keepdims=True)
    return center * lax.rsqrt(spread + EPSILON) * gain


def dot(a, b):
    return jnp.dot(a, b, preferred_element_type=jnp.float32)


MATS = ("pack", "p_lat", "p_halo", "back", "f_lat", "f_att", "f_ret", "out")


def kernel(info, heads, lon_size, lat_size, *refs):
    (nw, inner, nc, sizes, starts, n1, n2, wide) = info
    (latent_h, g1, wqkv_h, bqkv, btab, bidx, wproj_h, g2, wfc1_h, bfc1, wfc2_h, gm, wred_h) = refs[:13]
    mats_h = refs[13:21]
    o_ref = refs[21]
    (lat, wqkv, wproj, wfc1, wfc2, wred) = refs[22:28]
    mats = dict(zip(MATS, refs[28:36]))
    (send1, recv1, send2, recv2, qkv, mixed, att, bias, last_bias, idx, tab, hid, inside, merged) = refs[36:50]
    (load_sem, s1, r1, s2, r2) = refs[50:55]
    m = dict(zip(MATS, range(7, 15)))
    dim = lat.shape[1]
    head = dim // heads
    group = 256 // head
    groups = heads // group

    me_lon, me_lat = lax.axis_index("lon"), lax.axis_index("lat")
    west, east = lax.rem(me_lon + lon_size - 1, lon_size), lax.rem(me_lon + 1, lon_size)
    north, south = lax.rem(me_lat + lat_size - 1, lat_size), lax.rem(me_lat + 1, lat_size)
    to1 = [(west, me_lat), (me_lon, north), (west, north)]
    to2 = [(east, me_lat), (me_lon, south), (east, south)]
    barrier = pltpu.get_barrier_semaphore()
    for lo, la in to1 + to2:
        pl.semaphore_signal(barrier, inc=1, device_id={"lon": lo, "lat": la}, device_id_type=MESH)

    loads = {}

    def load(name, src, dst, n):
        loads[name] = pltpu.make_async_copy(src, dst, load_sem.at[n])
        loads[name].start()

    load("lat", latent_h, lat, 0)
    hbm = dict(zip(MATS, mats_h))
    load("pack", hbm["pack"], mats["pack"], m["pack"])
    load("p_lat", hbm["p_lat"], mats["p_lat"], m["p_lat"])
    load("wqkv", wqkv_h, wqkv, 1)
    load("p_halo", hbm["p_halo"], mats["p_halo"], m["p_halo"])
    load("wproj", wproj_h, wproj, 2)
    for name in ("back", "f_lat", "f_att"):
        load(name, hbm[name], mats[name], m[name])
    load("wfc1", wfc1_h, wfc1, 3)
    load("wfc2", wfc2_h, wfc2, 4)
    for name in ("f_ret", "out"):
        load(name, hbm[name], mats[name], m[name])
    load("wred", wred_h, wred, 5)

    def copies(src, dst, ss, rs, to):
        return [
            pltpu.make_async_remote_copy(
                src_ref=src.at[pl.ds(starts[k], sizes[k])],
                dst_ref=dst.at[pl.ds(starts[k], sizes[k])],
                send_sem=ss.at[k],
                recv_sem=rs.at[k],
                device_id={"lon": to[k][0], "lat": to[k][1]},
                device_id_type=MESH,
            )
            for k in range(3)
        ]

    loads["lat"].wait()
    loads["pack"].wait()
    send1[...] = dot(mats["pack"][...], lat[...]).astype(jnp.bfloat16)
    pl.semaphore_wait(barrier, 6)
    first = copies(send1, recv1, s1, r1, to1)
    for c in first:
        c.start()

    tab[...] = jnp.zeros_like(tab)
    tab[0 : btab.shape[0], 0:heads] = btab[...]
    idx[...] = jnp.zeros_like(idx)
    idx[0:WT, 0:WT] = bidx[...]
    lines = tab[...].T
    where = idx[...]
    low, high = jnp.bitwise_and(where, 127), where >= 128
    lane = lax.broadcasted_iota(jnp.int32, (WP, 128), 1)
    row = lax.broadcasted_iota(jnp.int32, (WP, 128), 0)
    other = jnp.where((row >= SH * WW) != (lane >= SH * WW), MASKED, 0.0)
    other = jnp.where(me_lat == lat_size - 1, other, 0.0)
    for h in range(heads):
        a = jnp.broadcast_to(lines[h : h + 1, 0:128], (WP, 128))
        b = jnp.broadcast_to(lines[h : h + 1, 128:256], (WP, 128))
        a = jnp.take_along_axis(a, low, axis=1, mode="promise_in_bounds")
        b = jnp.take_along_axis(b, low, axis=1, mode="promise_in_bounds")
        value = jnp.where(lane < WT, jnp.where(high, b, a), MASKED)
        bias[h * WP : (h + 1) * WP, :] = value
        last_bias[h * WP : (h + 1) * WP, :] = value + other

    lanes = lax.broadcasted_iota(jnp.int32, (1, 256), 1)
    picks = [
        jnp.where((lanes >= k * head) & (lanes < (k + 1) * head), head**-0.5, 0.0).astype(jnp.bfloat16)
        for k in range(group)
    ]

    def project(at, rows, tokens):
        normed = norm(tokens, g1[...]).astype(jnp.bfloat16)
        qkv[at : at + rows, :] = (dot(normed, wqkv[...]) + bqkv[...]).astype(jnp.bfloat16)

    def attend(w, table):
        at = pl.multiple_of(w * WP, 16)
        for g in range(groups):
            col = g * 256
            q = qkv[pl.ds(at, WP), col : col + 256]
            k = qkv[pl.ds(at, 128), dim + col : dim + col + 256]
            v = qkv[pl.ds(at, 128), 2 * dim + col : 2 * dim + col + 256]
            stacked = jnp.concatenate([q * p for p in picks], axis=0)
            scores = lax.dot_general(
                stacked, k, (((1,), (1,)), ((), ())), preferred_element_type=jnp.float32
            )
            scores = scores + table[g * group * WP : (g + 1) * group * WP, :]
            e = jnp.exp(scores - jnp.max(scores, axis=-1, keepdims=True))
            weights = (e * (1.0 / jnp.sum(e, axis=-1, keepdims=True))).astype(jnp.bfloat16)
            full = dot(weights, v)
            total = full[0:WP]
            for n in range(1, group):
                total = jnp.where(lanes >= n * head, full[n * WP : (n + 1) * WP], total)
            mixed[pl.ds(at, WP), col : col + 256] = total.astype(jnp.bfloat16)

    def attend_range(lo, hi, table):
        def body(w, carry):
            attend(w, table)
            return carry

        lax.fori_loop(lo, hi, body, 0)

    cut, end = inner * WP, nw * WP
    loads["p_lat"].wait()
    loads["wqkv"].wait()
    qkv[cut : cut + 48, :] = jnp.zeros((48, 3 * dim), jnp.bfloat16)
    qkv[end : end + 48, :] = jnp.zeros((48, 3 * dim), jnp.bfloat16)
    project(0, cut, dot(mats["p_lat"][0:cut, :], lat[...]))
    attend_range(0, inner, bias)
    loads["wproj"].wait()
    att[0:cut, :] = dot(mixed[0:cut, :], wproj[...]).astype(jnp.bfloat16)

    loads["p_halo"].wait()
    for c in first:
        c.wait()
    project(cut, end - cut, dot(mats["p_lat"][cut:end, :], lat[...]) + dot(mats["p_halo"][...], recv1[...]))
    attend_range(inner, nw - nc, bias)
    attend_range(nw - nc, nw, last_bias)
    att[cut:end, :] = dot(mixed[cut:end, :], wproj[...]).astype(jnp.bfloat16)
    loads["back"].wait()
    send2[...] = dot(mats["back"][...], att[cut:end, :]).astype(jnp.bfloat16)
    second = copies(send2, recv2, s2, r2, to2)
    for c in second:
        c.start()

    loads["f_lat"].wait()
    loads["f_att"].wait()
    loads["wfc1"].wait()
    loads["wfc2"].wait()

    def feed(at, rows, hidden):
        normed = norm(hidden, g2[...]).astype(jnp.bfloat16)
        hid[0:rows, :] = hidden
        step = 512
        for c in range(0, wfc1.shape[1], step):
            x = dot(normed, wfc1[:, c : c + step]) + bfc1[:, c : c + step]
            x = 0.5 * x * (1.0 + lax.erf(x * 0.7071067811865476))
            inside[0:rows, c : c + step] = x.astype(jnp.bfloat16)
        block = (hid[0:rows, :] + dot(inside[0:rows, :], wfc2[...])).astype(jnp.bfloat16).astype(jnp.float32)
        n = rows // 4
        parts = [block[q * n : (q + 1) * n] for q in range(4)]
        mean = sum(jnp.sum(p, axis=-1, keepdims=True) for p in parts) * (1.0 / (4 * dim))
        parts = [p - mean for p in parts]
        spread = sum(jnp.sum(p * p, axis=-1, keepdims=True) for p in parts) * (1.0 / (4 * dim))
        inv = lax.rsqrt(spread + EPSILON)
        for q, p in enumerate(parts):
            cols = slice(q * dim, (q + 1) * dim)
            merged[at : at + n, cols] = (p * inv * gm[:, cols]).astype(jnp.bfloat16)

    mid = 4 * n1
    feed(0, mid, dot(mats["f_lat"][0:mid, :], lat[...]) + dot(mats["f_att"][0:mid, :], att[...]))
    loads["f_ret"].wait()
    for c in second:
        c.wait()
    hidden = dot(mats["f_lat"][mid:, :], lat[...]) + (
        dot(mats["f_att"][mid:, :], att[...]) + dot(mats["f_ret"][...], recv2[...])
    )
    feed(n1, 4 * n2, hidden)
    loads["wred"].wait()
    loads["out"].wait()
    coarse = dot(merged[...], wred[...]).astype(jnp.bfloat16)
    o_ref[...] = dot(mats["out"][...], coarse).astype(jnp.bfloat16)


def per_device(lon_size, lat_size, latent, g1, wqkv, bqkv, btab, bidx, wproj, g2, wfc1, bfc1, wfc2, gm, wred):
    tr, tc, dim = latent.shape
    heads = btab.shape[1]
    mats, nw, inner, nc, sizes, starts, n1, n2, wide = plan(tr, tc)
    info = (nw, inner, nc, sizes, starts, n1, n2, wide)
    own, halo, rows = tr * tc, sum(sizes), nw * WP
    coarse = own // 4
    bf, f32 = jnp.bfloat16, jnp.float32
    any_ = pl.BlockSpec(memory_space=pl.ANY)
    vm = pl.BlockSpec(memory_space=pltpu.VMEM)
    vectors = {1, 3, 4, 5, 7, 9, 11}
    args = [latent.reshape(own, dim), g1[None], wqkv, bqkv[None], btab, bidx, wproj, g2[None], wfc1, bfc1[None], wfc2, gm[None], wred]
    args += [jnp.asarray(mats[k]) for k in MATS]
    specs = [vm if n in vectors else any_ for n in range(len(args))]
    scratch = [pltpu.VMEM(args[n].shape, bf) for n in (0, 2, 6, 8, 10, 12)]
    scratch += [pltpu.VMEM(mats[k].shape, bf) for k in MATS]
    scratch += [pltpu.VMEM((halo, dim), bf)] * 4
    scratch += [
        pltpu.VMEM((rows + 48, 3 * dim), bf),
        pltpu.VMEM((rows, dim), bf),
        pltpu.VMEM((rows, dim), bf),
        pltpu.VMEM((heads * WP, 128), f32),
        pltpu.VMEM((heads * WP, 128), f32),
        pltpu.VMEM((WP, 128), jnp.int32),
        pltpu.VMEM((256, 128), f32),
        pltpu.VMEM((4 * max(n1, n2), dim), f32),
        pltpu.VMEM((4 * max(n1, n2), wfc1.shape[1]), bf),
        pltpu.VMEM((coarse, 4 * dim), bf),
        pltpu.SemaphoreType.DMA((15,)),
        pltpu.SemaphoreType.DMA((3,)),
        pltpu.SemaphoreType.DMA((3,)),
        pltpu.SemaphoreType.DMA((3,)),
        pltpu.SemaphoreType.DMA((3,)),
    ]
    result = pl.pallas_call(
        functools.partial(kernel, info, heads, lon_size, lat_size),
        out_shape=jax.ShapeDtypeStruct((tr // 2 * wide, 2 * dim), bf),
        in_specs=specs,
        out_specs=vm,
        scratch_shapes=scratch,
        compiler_params=pltpu.CompilerParams(
            collective_id=0, has_side_effects=True, vmem_limit_bytes=56 * 1024 * 1024
        ),
        cost_estimate=pl.CostEstimate(flops=5 * 10**9, bytes_accessed=15 * 10**6, transcendentals=2 * 10**6),
    )(*args)
    return result.reshape(tr // 2, wide, 2 * dim)[:, : tc // 2]


def solution(mesh):
    in_specs = (P("lat", "lon", None),) + (P(),) * 12
    return jax.shard_map(
        functools.partial(per_device, mesh.shape["lon"], mesh.shape["lat"]),
        mesh=mesh,
        in_specs=in_specs,
        out_specs=P("lat", "lon", None),
        check_vma=False,
    )
```

```python
import functools

import jax
import jax.numpy as jnp
import numpy as np
from jax import lax
from jax.experimental import pallas as pl
from jax.experimental.pallas import tpu as pltpu
from jax.sharding import PartitionSpec as P

WH = 6
WW = 12
SH = 3
SW = 6
WT = WH * WW
WP = 80

EPSILON = 1e-05
MASKED = -1e30
MESH = pl.DeviceIdType.MESH


def up16(n):
    return (n + 15) // 16 * 16


def one_hot(rows, cols, pairs):
    out = np.zeros((rows, cols), np.float32)
    for r, c in pairs:
        out[r, c] = 1.0
    return out.astype(jnp.bfloat16)


@functools.lru_cache(None)
def plan(tr, tc):
    nb, nc = tr // WH, tc // WW
    windows = [(b, c) for b in range(nb - 1) for c in range(nc - 1)]
    inner = len(windows)
    windows += [(b, nc - 1) for b in range(nb - 1)]
    windows += [(nb - 1, c) for c in range(nc)]
    slot = {}
    for w, (b, c) in enumerate(windows):
        for r in range(WH):
            for k in range(WW):
                slot[b * WH + r, c * WW + k] = w * WP + r * WW + k
    east = [(i, j) for i in range(SH, tr) for j in range(SW)]
    south = [(i, j) for i in range(SH) for j in range(SW, tc)]
    corner = [(i, j) for i in range(SH) for j in range(SW)]
    sizes = [up16(len(x)) for x in (east, south, corner)]
    starts = [0, sizes[0], sizes[0] + sizes[1]]
    halo = sum(sizes)
    packed = {}
    for s, x in zip(starts, (east, south, corner)):
        for n, cell in enumerate(x):
            packed[cell] = s + n
    own = tr * tc
    pack = one_hot(halo, own, [(v, i * tc + j) for (i, j), v in packed.items()])
    rows = len(windows) * WP
    p_lat, p_halo, back = [], [], []
    for (i, j), s in slot.items():
        gi, gj = i + SH, j + SW
        wi, wj = gi % tr, gj % tc
        if gi < tr and gj < tc:
            p_lat.append((s, gi * tc + gj))
        else:
            p_halo.append((s, packed[wi, wj]))
            back.append((packed[wi, wj], s - inner * WP))
    p_lat = one_hot(rows, own, p_lat)
    p_halo = one_hot(rows, halo, p_halo)[inner * WP:]
    back = one_hot(halo, rows - inner * WP, back)
    first_r, first_c = -(-SH // 2), -(-SW // 2)
    cells = [(a, b) for a in range(tr // 2) for b in range(tc // 2)]
    free = [x for x in cells if x[0] >= first_r and x[1] >= first_c]
    n1 = len(free) // 16 * 16
    order = free + [x for x in cells if x not in set(free)]
    n2 = len(order) - n1
    f_lat, f_att, f_ret = [], [], []
    for n, (a, b) in enumerate(order):
        for q in range(4):
            i, j = 2 * a + q % 2, 2 * b + q // 2
            t = q * n1 + n if n < n1 else 4 * n1 + q * n2 + n - n1
            f_lat.append((t, i * tc + j))
            if i >= SH and j >= SW:
                f_att.append((t, slot[i - SH, j - SW]))
            else:
                f_ret.append((t - 4 * n1, packed[i, j]))
    f_lat = one_hot(own, own, f_lat)
    f_att = one_hot(own, rows, f_att)
    f_ret = one_hot(4 * n2, halo, f_ret)
    wide = up16(tc // 2)
    out = one_hot(tr // 2 * wide, len(order), [(a * wide + b, n) for n, (a, b) in enumerate(order)])
    mats = dict(pack=pack, p_lat=p_lat, p_halo=p_halo, back=back, f_lat=f_lat, f_att=f_att, f_ret=f_ret, out=out)
    return mats, len(windows), inner, nc, sizes, starts, n1, n2, wide


def norm(values, gain):
    center = values - jnp.mean(values, axis=-1, keepdims=True)
    spread = jnp.mean(center * center, axis=-1, keepdims=True)
    return center * lax.rsqrt(spread + EPSILON) * gain


def dot(a, b):
    return jnp.dot(a, b, preferred_element_type=jnp.float32)


MATS = ("pack", "p_lat", "p_halo", "back", "f_lat", "f_att", "f_ret", "out")


def kernel(info, heads, lon_size, lat_size, *refs):
    (nw, inner, nc, sizes, starts, n1, n2, wide) = info
    (latent_h, g1, wqkv_h, bqkv, btab, bidx, wproj_h, g2, wfc1_h, bfc1, wfc2_h, gm, wred_h) = refs[:13]
    mats_h = refs[13:21]
    o_ref = refs[21]
    (lat, wqkv, wproj, wfc1, wfc2, wred) = refs[22:28]
    mats = dict(zip(MATS, refs[28:36]))
    (send1, recv1, send2, recv2, qkv, mixed, att, bias, last_bias, idx, tab, hid, inside, merged) = refs[36:50]
    (load_sem, s1, r1, s2, r2) = refs[50:55]
    m = dict(zip(MATS, range(7, 15)))
    dim = lat.shape[1]
    head = dim // heads
    group = 256 // head
    groups = heads // group

    me_lon, me_lat = lax.axis_index("lon"), lax.axis_index("lat")
    west, east = lax.rem(me_lon + lon_size - 1, lon_size), lax.rem(me_lon + 1, lon_size)
    north, south = lax.rem(me_lat + lat_size - 1, lat_size), lax.rem(me_lat + 1, lat_size)
    to1 = [(west, me_lat), (me_lon, north), (west, north)]
    to2 = [(east, me_lat), (me_lon, south), (east, south)]
    barrier = pltpu.get_barrier_semaphore()
    for lo, la in to1 + to2:
        pl.semaphore_signal(barrier, inc=1, device_id={"lon": lo, "lat": la}, device_id_type=MESH)

    loads = {}

    def load(name, src, dst, n):
        loads[name] = pltpu.make_async_copy(src, dst, load_sem.at[n])
        loads[name].start()

    load("lat", latent_h, lat, 0)
    hbm = dict(zip(MATS, mats_h))
    load("pack", hbm["pack"], mats["pack"], m["pack"])
    load("p_lat", hbm["p_lat"], mats["p_lat"], m["p_lat"])
    load("wqkv", wqkv_h, wqkv, 1)
    load("p_halo", hbm["p_halo"], mats["p_halo"], m["p_halo"])
    load("wproj", wproj_h, wproj, 2)
    for name in ("back", "f_lat", "f_att"):
        load(name, hbm[name], mats[name], m[name])
    load("wfc1", wfc1_h, wfc1, 3)
    load("wfc2", wfc2_h, wfc2, 4)
    for name in ("f_ret", "out"):
        load(name, hbm[name], mats[name], m[name])
    load("wred", wred_h, wred, 5)

    def copies(src, dst, ss, rs, to):
        return [
            pltpu.make_async_remote_copy(
                src_ref=src.at[pl.ds(starts[k], sizes[k])],
                dst_ref=dst.at[pl.ds(starts[k], sizes[k])],
                send_sem=ss.at[k],
                recv_sem=rs.at[k],
                device_id={"lon": to[k][0], "lat": to[k][1]},
                device_id_type=MESH,
            )
            for k in range(3)
        ]

    loads["lat"].wait()
    loads["pack"].wait()
    send1[...] = dot(mats["pack"][...], lat[...]).astype(jnp.bfloat16)
    pl.semaphore_wait(barrier, 6)
    first = copies(send1, recv1, s1, r1, to1)
    for c in first:
        c.start()

    tab[...] = jnp.zeros_like(tab)
    tab[0:heads, 0 : btab.shape[1]] = btab[...]
    idx[...] = jnp.zeros_like(idx)
    idx[0:WT, 0:WT] = bidx[...]
    lines = tab[...]
    where = idx[...]
    low, high = jnp.bitwise_and(where, 127), where >= 128
    lane = lax.broadcasted_iota(jnp.int32, (WP, 128), 1)
    row = lax.broadcasted_iota(jnp.int32, (WP, 128), 0)
    other = jnp.where((row >= SH * WW) != (lane >= SH * WW), MASKED, 0.0)
    other = jnp.where(me_lat == lat_size - 1, other, 0.0)
    for h in range(heads):
        a = jnp.broadcast_to(lines[h : h + 1, 0:128], (WP, 128))
        b = jnp.broadcast_to(lines[h : h + 1, 128:256], (WP, 128))
        a = jnp.take_along_axis(a, low, axis=1, mode="promise_in_bounds")
        b = jnp.take_along_axis(b, low, axis=1, mode="promise_in_bounds")
        value = jnp.where(lane < WT, jnp.where(high, b, a), MASKED)
        bias[h * WP : (h + 1) * WP, :] = value
        last_bias[h * WP : (h + 1) * WP, :] = value + other

    lanes = lax.broadcasted_iota(jnp.int32, (1, 256), 1)
    picks = [
        jnp.where((lanes >= k * head) & (lanes < (k + 1) * head), head**-0.5, 0.0).astype(jnp.bfloat16)
        for k in range(group)
    ]

    def project(at, rows, tokens):
        normed = norm(tokens, g1[...]).astype(jnp.bfloat16)
        qkv[at : at + rows, :] = (dot(normed, wqkv[...]) + bqkv[...][None, :]).astype(jnp.bfloat16)

    def attend(w, table):
        at = w * WP
        for g in range(groups):
            col = g * 256
            q = qkv[pl.ds(at, WP), col : col + 256]
            k = qkv[pl.ds(at, 128), dim + col : dim + col + 256]
            v = qkv[pl.ds(at, 128), 2 * dim + col : 2 * dim + col + 256]
            stacked = jnp.concatenate([q * p for p in picks], axis=0)
            scores = lax.dot_general(
                stacked, k, (((1,), (1,)), ((), ())), preferred_element_type=jnp.float32
            )
            scores = scores + table[g * group * WP : (g + 1) * group * WP, :]
            e = jnp.exp(scores - jnp.max(scores, axis=-1, keepdims=True))
            weights = (e * (1.0 / jnp.sum(e, axis=-1, keepdims=True))).astype(jnp.bfloat16)
            full = dot(weights, v)
            total = full[0:WP]
            for n in range(1, group):
                total = jnp.where(lanes >= n * head, full[n * WP : (n + 1) * WP], total)
            mixed[pl.ds(at, WP), col : col + 256] = total.astype(jnp.bfloat16)

    def attend_range(lo, hi, table):
        for w in range(lo, hi):
            attend(w, table)

    cut, end = inner * WP, nw * WP
    loads["p_lat"].wait()
    loads["wqkv"].wait()
    qkv[cut : cut + 48, :] = jnp.zeros((48, 3 * dim), jnp.bfloat16)
    qkv[end : end + 48, :] = jnp.zeros((48, 3 * dim), jnp.bfloat16)
    project(0, cut, dot(mats["p_lat"][0:cut, :], lat[...]))
    attend_range(0, inner, bias)
    loads["wproj"].wait()
    att[0:cut, :] = dot(mixed[0:cut, :], wproj[...]).astype(jnp.bfloat16)

    loads["p_halo"].wait()
    for c in first:
        c.wait()
    project(cut, end - cut, dot(mats["p_lat"][cut:end, :], lat[...]) + dot(mats["p_halo"][...], recv1[...]))
    attend_range(inner, nw - nc, bias)
    attend_range(nw - nc, nw, last_bias)
    att[cut:end, :] = dot(mixed[cut:end, :], wproj[...]).astype(jnp.bfloat16)
    loads["back"].wait()
    send2[...] = dot(mats["back"][...], att[cut:end, :]).astype(jnp.bfloat16)
    second = copies(send2, recv2, s2, r2, to2)
    for c in second:
        c.start()

    loads["f_lat"].wait()
    loads["f_att"].wait()
    loads["wfc1"].wait()
    loads["wfc2"].wait()

    def feed(at, rows, hidden):
        normed = norm(hidden, g2[...]).astype(jnp.bfloat16)
        hid[0:rows, :] = hidden
        step = 512
        for c in range(0, wfc1.shape[1], step):
            x = dot(normed, wfc1[:, c : c + step]) + bfc1[:, c : c + step]
            x = 0.5 * x * (1.0 + lax.erf(x * 0.7071067811865476))
            inside[0:rows, c : c + step] = x.astype(jnp.bfloat16)
        block = (hid[0:rows, :] + dot(inside[0:rows, :], wfc2[...])).astype(jnp.bfloat16).astype(jnp.float32)
        n = rows // 4
        parts = [block[q * n : (q + 1) * n] for q in range(4)]
        mean = sum(jnp.sum(p, axis=-1, keepdims=True) for p in parts) * (1.0 / (4 * dim))
        parts = [p - mean for p in parts]
        spread = sum(jnp.sum(p * p, axis=-1, keepdims=True) for p in parts) * (1.0 / (4 * dim))
        inv = lax.rsqrt(spread + EPSILON)
        for q, p in enumerate(parts):
            cols = slice(q * dim, (q + 1) * dim)
            merged[at : at + n, cols] = (p * inv * gm[:, cols]).astype(jnp.bfloat16)

    mid = 4 * n1
    feed(0, mid, dot(mats["f_lat"][0:mid, :], lat[...]) + dot(mats["f_att"][0:mid, :], att[...]))
    loads["f_ret"].wait()
    for c in second:
        c.wait()
    hidden = dot(mats["f_lat"][mid:, :], lat[...]) + (
        dot(mats["f_att"][mid:, :], att[...]) + dot(mats["f_ret"][...], recv2[...])
    )
    feed(n1, 4 * n2, hidden)
    loads["wred"].wait()
    loads["out"].wait()
    coarse = dot(merged[...], wred[...]).astype(jnp.bfloat16)
    o_ref[...] = dot(mats["out"][...], coarse).astype(jnp.bfloat16)


def per_device(lon_size, lat_size, latent, g1, wqkv, bqkv, btab, bidx, wproj, g2, wfc1, bfc1, wfc2, gm, wred):
    tr, tc, dim = latent.shape
    heads = btab.shape[1]
    mats, nw, inner, nc, sizes, starts, n1, n2, wide = plan(tr, tc)
    info = (nw, inner, nc, sizes, starts, n1, n2, wide)
    own, halo, rows = tr * tc, sum(sizes), nw * WP
    coarse = own // 4
    bf, f32 = jnp.bfloat16, jnp.float32
    any_ = pl.BlockSpec(memory_space=pl.ANY)
    vm = pl.BlockSpec(memory_space=pltpu.VMEM)
    vectors = {1, 3, 4, 5, 7, 9, 11}
    args = [latent.reshape(own, dim), g1[None], wqkv, bqkv, btab.T, bidx, wproj, g2[None], wfc1, bfc1[None], wfc2, gm[None], wred]
    args += [jnp.asarray(mats[k]) for k in MATS]
    specs = [vm if n in vectors else any_ for n in range(len(args))]
    scratch = [pltpu.VMEM(args[n].shape, bf) for n in (0, 2, 6, 8, 10, 12)]
    scratch += [pltpu.VMEM(mats[k].shape, bf) for k in MATS]
    scratch += [pltpu.VMEM((halo, dim), bf)] * 4
    scratch += [
        pltpu.VMEM((rows + 48, 3 * dim), bf),
        pltpu.VMEM((rows, dim), bf),
        pltpu.VMEM((rows, dim), bf),
        pltpu.VMEM((heads * WP, 128), f32),
        pltpu.VMEM((heads * WP, 128), f32),
        pltpu.VMEM((WP, 128), jnp.int32),
        pltpu.VMEM((heads, 256), f32),
        pltpu.VMEM((4 * max(n1, n2), dim), f32),
        pltpu.VMEM((4 * max(n1, n2), wfc1.shape[1]), bf),
        pltpu.VMEM((coarse, 4 * dim), bf),
        pltpu.SemaphoreType.DMA((15,)),
        pltpu.SemaphoreType.DMA((3,)),
        pltpu.SemaphoreType.DMA((3,)),
        pltpu.SemaphoreType.DMA((3,)),
        pltpu.SemaphoreType.DMA((3,)),
    ]
    result = pl.pallas_call(
        functools.partial(kernel, info, heads, lon_size, lat_size),
        out_shape=jax.ShapeDtypeStruct((tr // 2 * wide, 2 * dim), bf),
        in_specs=specs,
        out_specs=vm,
        scratch_shapes=scratch,
        compiler_params=pltpu.CompilerParams(
            collective_id=0, has_side_effects=True, vmem_limit_bytes=56 * 1024 * 1024
        ),
        cost_estimate=pl.CostEstimate(flops=5 * 10**9, bytes_accessed=15 * 10**6, transcendentals=2 * 10**6),
    )(*args)
    return result.reshape(tr // 2, wide, 2 * dim)[:, : tc // 2]


def solution(mesh):
    in_specs = (P("lat", "lon", None),) + (P(),) * 12
    return jax.shard_map(
        functools.partial(per_device, mesh.shape["lon"], mesh.shape["lat"]),
        mesh=mesh,
        in_specs=in_specs,
        out_specs=P("lat", "lon", None),
        check_vma=False,
    )
```

```python
import functools

import jax
import jax.numpy as jnp
import numpy as np
from jax import lax
from jax.experimental import pallas as pl
from jax.experimental.pallas import tpu as pltpu
from jax.sharding import PartitionSpec as P

WH = 6
WW = 12
SH = 3
SW = 6
WT = WH * WW
WP = 80

EPSILON = 1e-05
MASKED = -1e30
MESH = pl.DeviceIdType.MESH


def up16(n):
    return (n + 15) // 16 * 16


def one_hot(rows, cols, pairs):
    out = np.zeros((rows, cols), np.float32)
    for r, c in pairs:
        out[r, c] = 1.0
    return out.astype(jnp.bfloat16)


@functools.lru_cache(None)
def plan(tr, tc):
    nb, nc = tr // WH, tc // WW
    windows = [(b, c) for b in range(nb - 1) for c in range(nc - 1)]
    inner = len(windows)
    windows += [(b, nc - 1) for b in range(nb - 1)]
    windows += [(nb - 1, c) for c in range(nc)]
    slot = {}
    for w, (b, c) in enumerate(windows):
        for r in range(WH):
            for k in range(WW):
                slot[b * WH + r, c * WW + k] = w * WP + r * WW + k
    east = [(i, j) for i in range(SH, tr) for j in range(SW)]
    south = [(i, j) for i in range(SH) for j in range(SW, tc)]
    corner = [(i, j) for i in range(SH) for j in range(SW)]
    sizes = [up16(len(x)) for x in (east, south, corner)]
    starts = [0, sizes[0], sizes[0] + sizes[1]]
    halo = sum(sizes)
    packed = {}
    for s, x in zip(starts, (east, south, corner)):
        for n, cell in enumerate(x):
            packed[cell] = s + n
    own = tr * tc
    pack = one_hot(halo, own, [(v, i * tc + j) for (i, j), v in packed.items()])
    rows = len(windows) * WP
    p_lat, p_halo, back = [], [], []
    for (i, j), s in slot.items():
        gi, gj = i + SH, j + SW
        wi, wj = gi % tr, gj % tc
        if gi < tr and gj < tc:
            p_lat.append((s, gi * tc + gj))
        else:
            p_halo.append((s, packed[wi, wj]))
            back.append((packed[wi, wj], s - inner * WP))
    p_lat = one_hot(rows, own, p_lat)
    p_halo = one_hot(rows, halo, p_halo)[inner * WP:]
    back = one_hot(halo, rows - inner * WP, back)
    first_r, first_c = -(-SH // 2), -(-SW // 2)
    cells = [(a, b) for a in range(tr // 2) for b in range(tc // 2)]
    free = [x for x in cells if x[0] >= first_r and x[1] >= first_c]
    n1 = len(free) // 16 * 16
    order = free + [x for x in cells if x not in set(free)]
    n2 = len(order) - n1
    f_lat, f_att, f_ret = [], [], []
    for n, (a, b) in enumerate(order):
        for q in range(4):
            i, j = 2 * a + q % 2, 2 * b + q // 2
            t = q * n1 + n if n < n1 else 4 * n1 + q * n2 + n - n1
            f_lat.append((t, i * tc + j))
            if i >= SH and j >= SW:
                f_att.append((t, slot[i - SH, j - SW]))
            else:
                f_ret.append((t - 4 * n1, packed[i, j]))
    f_lat = one_hot(own, own, f_lat)
    f_att = one_hot(own, rows, f_att)
    f_ret = one_hot(4 * n2, halo, f_ret)
    wide = up16(tc // 2)
    out = one_hot(tr // 2 * wide, len(order), [(a * wide + b, n) for n, (a, b) in enumerate(order)])
    mats = dict(pack=pack, p_lat=p_lat, p_halo=p_halo, back=back, f_lat=f_lat, f_att=f_att, f_ret=f_ret, out=out)
    return mats, len(windows), inner, nc, sizes, starts, n1, n2, wide


def norm(values, gain):
    center = values - jnp.mean(values, axis=-1, keepdims=True)
    spread = jnp.mean(center * center, axis=-1, keepdims=True)
    return center * lax.rsqrt(spread + EPSILON) * gain


def dot(a, b):
    return jnp.dot(a, b, preferred_element_type=jnp.float32)


MATS = ("pack", "p_lat", "p_halo", "back", "f_lat", "f_att", "f_ret", "out")


def kernel(info, heads, lon_size, lat_size, *refs):
    (nw, inner, nc, sizes, starts, n1, n2, wide) = info
    (latent_h, g1, wqkv_h, bqkv, btab, bidx, wproj_h, g2, wfc1_h, bfc1, wfc2_h, gm, wred_h) = refs[:13]
    mats_h = refs[13:21]
    o_ref = refs[21]
    (lat, wqkv, wproj, wfc1, wfc2, wred) = refs[22:28]
    mats = dict(zip(MATS, refs[28:36]))
    (send1, recv1, send2, recv2, qkv, mixed, att, bias, last_bias, idx, tab, hid, inside, merged, local) = refs[36:51]
    (load_sem, s1, r1, s2, r2) = refs[51:56]
    m = dict(zip(MATS, range(7, 15)))
    dim = lat.shape[1]
    head = dim // heads
    group = 256 // head
    groups = heads // group

    me_lon, me_lat = lax.axis_index("lon"), lax.axis_index("lat")
    west, east = lax.rem(me_lon + lon_size - 1, lon_size), lax.rem(me_lon + 1, lon_size)
    north, south = lax.rem(me_lat + lat_size - 1, lat_size), lax.rem(me_lat + 1, lat_size)
    to1 = [(west, me_lat), (me_lon, north), (west, north)]
    to2 = [(east, me_lat), (me_lon, south), (east, south)]
    barrier = pltpu.get_barrier_semaphore()
    for lo, la in to1 + to2:
        pl.semaphore_signal(barrier, inc=1, device_id={"lon": lo, "lat": la}, device_id_type=MESH)

    loads = {}

    def load(name, src, dst, n):
        loads[name] = pltpu.make_async_copy(src, dst, load_sem.at[n])
        loads[name].start()

    load("lat", latent_h, lat, 0)
    hbm = dict(zip(MATS, mats_h))
    load("pack", hbm["pack"], mats["pack"], m["pack"])
    load("p_lat", hbm["p_lat"], mats["p_lat"], m["p_lat"])
    load("wqkv", wqkv_h, wqkv, 1)
    load("p_halo", hbm["p_halo"], mats["p_halo"], m["p_halo"])
    load("wproj", wproj_h, wproj, 2)
    for name in ("back", "f_lat", "f_att"):
        load(name, hbm[name], mats[name], m[name])
    load("wfc1", wfc1_h, wfc1, 3)
    load("wfc2", wfc2_h, wfc2, 4)
    for name in ("f_ret", "out"):
        load(name, hbm[name], mats[name], m[name])
    load("wred", wred_h, wred, 5)

    def copies(src, dst, ss, rs, to):
        return [
            pltpu.make_async_remote_copy(
                src_ref=src.at[pl.ds(starts[k], sizes[k])],
                dst_ref=dst.at[pl.ds(starts[k], sizes[k])],
                send_sem=ss.at[k],
                recv_sem=rs.at[k],
                device_id={"lon": to[k][0], "lat": to[k][1]},
                device_id_type=MESH,
            )
            for k in range(3)
        ]

    loads["lat"].wait()
    loads["pack"].wait()
    send1[...] = dot(mats["pack"][...], lat[...]).astype(jnp.bfloat16)
    pl.semaphore_wait(barrier, 6)
    first = copies(send1, recv1, s1, r1, to1)
    for c in first:
        c.start()

    tab[...] = jnp.zeros_like(tab)
    tab[0:heads, 0 : btab.shape[1]] = btab[...]
    idx[...] = jnp.zeros_like(idx)
    idx[0:WT, 0:WT] = bidx[...]
    lines = tab[...]
    where = idx[...]
    low, high = jnp.bitwise_and(where, 127), where >= 128
    lane = lax.broadcasted_iota(jnp.int32, (WP, 128), 1)
    row = lax.broadcasted_iota(jnp.int32, (WP, 128), 0)
    other = jnp.where((row >= SH * WW) != (lane >= SH * WW), MASKED, 0.0)
    other = jnp.where(me_lat == lat_size - 1, other, 0.0)
    for h in range(heads):
        a = jnp.broadcast_to(lines[h : h + 1, 0:128], (WP, 128))
        b = jnp.broadcast_to(lines[h : h + 1, 128:256], (WP, 128))
        a = jnp.take_along_axis(a, low, axis=1, mode="promise_in_bounds")
        b = jnp.take_along_axis(b, low, axis=1, mode="promise_in_bounds")
        value = jnp.where(lane < WT, jnp.where(high, b, a), MASKED)
        bias[h * WP : (h + 1) * WP, :] = value
        last_bias[h * WP : (h + 1) * WP, :] = value + other

    lanes = lax.broadcasted_iota(jnp.int32, (1, 256), 1)
    picks = [
        jnp.where((lanes >= k * head) & (lanes < (k + 1) * head), head**-0.5, 0.0).astype(jnp.bfloat16)
        for k in range(group)
    ]

    def project(at, rows, tokens):
        normed = norm(tokens, g1[...]).astype(jnp.bfloat16)
        qkv[at : at + rows, :] = (dot(normed, wqkv[...]) + bqkv[...][None, :]).astype(jnp.bfloat16)

    def attend(w, table):
        at = w * WP
        for g in range(groups):
            col = g * 256
            q = qkv[pl.ds(at, WP), col : col + 256]
            k = qkv[pl.ds(at, 128), dim + col : dim + col + 256]
            v = qkv[pl.ds(at, 128), 2 * dim + col : 2 * dim + col + 256]
            stacked = jnp.concatenate([q * p for p in picks], axis=0)
            scores = lax.dot_general(
                stacked, k, (((1,), (1,)), ((), ())), preferred_element_type=jnp.float32
            )
            scores = scores + table[g * group * WP : (g + 1) * group * WP, :]
            e = jnp.exp(scores - jnp.max(scores, axis=-1, keepdims=True))
            weights = (e * (1.0 / jnp.sum(e, axis=-1, keepdims=True))).astype(jnp.bfloat16)
            full = dot(weights, v)
            total = full[0:WP]
            for n in range(1, group):
                total = jnp.where(lanes >= n * head, full[n * WP : (n + 1) * WP], total)
            mixed[pl.ds(at, WP), col : col + 256] = total.astype(jnp.bfloat16)

    def attend_range(lo, hi, table):
        for w in range(lo, hi):
            attend(w, table)

    cut, end = inner * WP, nw * WP
    loads["p_lat"].wait()
    loads["wqkv"].wait()
    qkv[cut : cut + 48, :] = jnp.zeros((48, 3 * dim), jnp.bfloat16)
    qkv[end : end + 48, :] = jnp.zeros((48, 3 * dim), jnp.bfloat16)
    project(0, cut, dot(mats["p_lat"][0:cut, :], lat[...]))
    attend_range(0, inner, bias)
    loads["wproj"].wait()
    att[0:cut, :] = dot(mixed[0:cut, :], wproj[...]).astype(jnp.bfloat16)

    local[...] = dot(mats["p_lat"][cut:end, :], lat[...])
    loads["p_halo"].wait()
    for c in first:
        c.wait()
    project(cut, end - cut, local[...] + dot(mats["p_halo"][...], recv1[...]))
    attend_range(inner, nw - nc, bias)
    attend_range(nw - nc, nw, last_bias)
    att[cut:end, :] = dot(mixed[cut:end, :], wproj[...]).astype(jnp.bfloat16)
    loads["back"].wait()
    send2[...] = dot(mats["back"][...], att[cut:end, :]).astype(jnp.bfloat16)
    second = copies(send2, recv2, s2, r2, to2)
    for c in second:
        c.start()

    loads["f_lat"].wait()
    loads["f_att"].wait()
    loads["wfc1"].wait()
    loads["wfc2"].wait()

    def feed(at, rows, hidden):
        normed = norm(hidden, g2[...]).astype(jnp.bfloat16)
        hid[0:rows, :] = hidden
        step = 512
        for c in range(0, wfc1.shape[1], step):
            x = dot(normed, wfc1[:, c : c + step]) + bfc1[:, c : c + step]
            x = 0.5 * x * (1.0 + lax.erf(x * 0.7071067811865476))
            inside[0:rows, c : c + step] = x.astype(jnp.bfloat16)
        block = (hid[0:rows, :] + dot(inside[0:rows, :], wfc2[...])).astype(jnp.bfloat16).astype(jnp.float32)
        n = rows // 4
        parts = [block[q * n : (q + 1) * n] for q in range(4)]
        mean = sum(jnp.sum(p, axis=-1, keepdims=True) for p in parts) * (1.0 / (4 * dim))
        parts = [p - mean for p in parts]
        spread = sum(jnp.sum(p * p, axis=-1, keepdims=True) for p in parts) * (1.0 / (4 * dim))
        inv = lax.rsqrt(spread + EPSILON)
        for q, p in enumerate(parts):
            cols = slice(q * dim, (q + 1) * dim)
            merged[at : at + n, cols] = (p * inv * gm[:, cols]).astype(jnp.bfloat16)

    mid = 4 * n1
    feed(0, mid, dot(mats["f_lat"][0:mid, :], lat[...]) + dot(mats["f_att"][0:mid, :], att[...]))
    local[0 : 4 * n2, :] = dot(mats["f_lat"][mid:, :], lat[...]) + dot(mats["f_att"][mid:, :], att[...])
    loads["f_ret"].wait()
    for c in second:
        c.wait()
    feed(n1, 4 * n2, local[0 : 4 * n2, :] + dot(mats["f_ret"][...], recv2[...]))
    loads["wred"].wait()
    loads["out"].wait()
    coarse = dot(merged[...], wred[...]).astype(jnp.bfloat16)
    o_ref[...] = dot(mats["out"][...], coarse).astype(jnp.bfloat16)


def per_device(lon_size, lat_size, latent, g1, wqkv, bqkv, btab, bidx, wproj, g2, wfc1, bfc1, wfc2, gm, wred):
    tr, tc, dim = latent.shape
    heads = btab.shape[1]
    mats, nw, inner, nc, sizes, starts, n1, n2, wide = plan(tr, tc)
    info = (nw, inner, nc, sizes, starts, n1, n2, wide)
    own, halo, rows = tr * tc, sum(sizes), nw * WP
    coarse = own // 4
    bf, f32 = jnp.bfloat16, jnp.float32
    any_ = pl.BlockSpec(memory_space=pl.ANY)
    vm = pl.BlockSpec(memory_space=pltpu.VMEM)
    vectors = {1, 3, 4, 5, 7, 9, 11}
    args = [latent.reshape(own, dim), g1[None], wqkv, bqkv, btab.T, bidx, wproj, g2[None], wfc1, bfc1[None], wfc2, gm[None], wred]
    args += [jnp.asarray(mats[k]) for k in MATS]
    specs = [vm if n in vectors else any_ for n in range(len(args))]
    scratch = [pltpu.VMEM(args[n].shape, bf) for n in (0, 2, 6, 8, 10, 12)]
    scratch += [pltpu.VMEM(mats[k].shape, bf) for k in MATS]
    scratch += [pltpu.VMEM((halo, dim), bf)] * 4
    scratch += [
        pltpu.VMEM((rows + 48, 3 * dim), bf),
        pltpu.VMEM((rows, dim), bf),
        pltpu.VMEM((rows, dim), bf),
        pltpu.VMEM((heads * WP, 128), f32),
        pltpu.VMEM((heads * WP, 128), f32),
        pltpu.VMEM((WP, 128), jnp.int32),
        pltpu.VMEM((heads, 256), f32),
        pltpu.VMEM((4 * max(n1, n2), dim), f32),
        pltpu.VMEM((4 * max(n1, n2), wfc1.shape[1]), bf),
        pltpu.VMEM((coarse, 4 * dim), bf),
        pltpu.VMEM((max(rows - inner * WP, 4 * n2), dim), f32),
        pltpu.SemaphoreType.DMA((15,)),
        pltpu.SemaphoreType.DMA((3,)),
        pltpu.SemaphoreType.DMA((3,)),
        pltpu.SemaphoreType.DMA((3,)),
        pltpu.SemaphoreType.DMA((3,)),
    ]
    result = pl.pallas_call(
        functools.partial(kernel, info, heads, lon_size, lat_size),
        out_shape=jax.ShapeDtypeStruct((tr // 2 * wide, 2 * dim), bf),
        in_specs=specs,
        out_specs=vm,
        scratch_shapes=scratch,
        compiler_params=pltpu.CompilerParams(
            collective_id=0, has_side_effects=True, vmem_limit_bytes=56 * 1024 * 1024
        ),
        cost_estimate=pl.CostEstimate(flops=5 * 10**9, bytes_accessed=15 * 10**6, transcendentals=2 * 10**6),
    )(*args)
    return result.reshape(tr // 2, wide, 2 * dim)[:, : tc // 2]


def solution(mesh):
    in_specs = (P("lat", "lon", None),) + (P(),) * 12
    return jax.shard_map(
        functools.partial(per_device, mesh.shape["lon"], mesh.shape["lat"]),
        mesh=mesh,
        in_specs=in_specs,
        out_specs=P("lat", "lon", None),
        check_vma=False,
    )
```
